32 devices in a mesh: row: 8 (over y, x, core), col: 4 (over z).
Axes of the slice: x: 2, y: 2, z: 4, core: 2. Of those that a mesh axis runs over, the one named last changes fastest.
Arguments:
- tokens: bfloat16 [512, 8192], P('col', 'row'), may hold values from -6 to 6
- cotangent: bfloat16 [512, 8192], P('col', 'row'), may hold values from -6 to 6
- gate_weight: bfloat16 [8192, 28672], P('row', 'col'), may hold values from -0.09375 to 0.09375
- up_weight: bfloat16 [8192, 28672], P('row', 'col'), may hold values from -0.09375 to 0.09375
- down_weight: bfloat16 [28672, 8192], P('col', 'row'), may hold values from -0.0625 to 0.0625
- gate_mask: int32 [64, 224], P('row', 'col'), may hold values 0 or 1
- up_mask: int32 [64, 224], P('row', 'col'), may hold values 0 or 1
- down_mask: int32 [224, 64], P('col', 'row'), may hold values 0 or 1
Outputs:
- output: bfloat16 [512, 8192], P('col', 'row')
- d_tokens: bfloat16 [512, 8192], P('col', 'row')
- grad_gate: bfloat16 [8192, 28672], P('row', 'col')
- grad_up: bfloat16 [8192, 28672], P('row', 'col')
- grad_down: bfloat16 [28672, 8192], P('col', 'row')
The draws below stay inside these ranges and needn't reach their ends.
Inputs may be any that keep to these rules, and one draw needn't show every extreme that they name: `gate_mask`: 1 keeps a block, 0 prunes it. `up_mask`: 1 keeps a block, 0 prunes it. `down_mask`: 1 keeps a block, 0 prunes it.
All inputs are finite; a program needn't handle non-finite values.
Results may differ from the reference program's by a relative error of at most 0.0049.
Values may be sent and summed in bfloat16 or wider, within the bound.
A program may use at most 256 MiB of HBM per device.

```python
import jax
import jax.numpy as jnp

D = 8192
HID = 28672
BLK = 128
TOKENS = 512


def place_ends(drawn, own_key, least, high):
    index_at = [jax.random.randint(jax.random.fold_in(own_key, axis), (), 0, length) for axis, length in enumerate(drawn.shape)]
    widest = drawn.shape.index(max(drawn.shape))
    neighbour = index_at[:widest] + [(index_at[widest] + 1) % drawn.shape[widest]] + index_at[widest + 1:]
    return drawn.at[tuple(index_at)].set(least).at[tuple(neighbour)].set(high)


def shard_levels(stream_key, extent, pieces, least, largest):
    level = 1.0
    for position, shards_of in pieces:
        draws = jax.random.uniform(jax.random.fold_in(jax.random.fold_in(stream_key, 6), position), (shards_of,), jnp.float32, least / len(pieces), largest / len(pieces))
        level = level * jnp.repeat(jnp.exp(draws), extent[position] // shards_of).reshape((-1,) + (1,) * (len(extent) - 1 - position))
    return level


def bell_draw(stream_key, shape, spread, most, pieces=(), kind=jnp.bfloat16):
    result = jax.random.normal(stream_key, shape, jnp.float32) * spread
    if len(pieces) > 0:
        result = shard_levels(stream_key, shape, pieces, -0.22, 0.18) * result
    return jnp.clip(result, min=-most, max=most).astype(kind)


def setup_inputs(seed: int = 0) -> dict:
    streams_of = jax.random.split(jax.random.key(seed), 9)
    return {
        "tokens": bell_draw(streams_of[0], (TOKENS, D), 1.0, 6.0, ((0, 4), (1, 8))),
        "cotangent": bell_draw(streams_of[1], (TOKENS, D), 1.0, 6.0, ((0, 4), (1, 8))),
        "gate_weight": bell_draw(streams_of[2], (D, HID), (D // 2) ** -0.5, 0.09375, ((0, 8), (1, 4))),
        "up_weight": bell_draw(streams_of[3], (D, HID), (D // 2) ** -0.5, 0.09375, ((0, 8), (1, 4))),
        "down_weight": bell_draw(streams_of[4], (HID, D), (HID // 4) ** -0.5, 0.0625, ((0, 4), (1, 8))),
        "gate_mask": place_ends((jax.random.randint(streams_of[5], (D // BLK, HID // BLK), 0, 2) < 1).astype(jnp.int32), jax.random.fold_in(streams_of[5], 1), 0, 1),
        "up_mask": place_ends((jax.random.randint(streams_of[6], (D // BLK, HID // BLK), 0, 2) < 1).astype(jnp.int32), jax.random.fold_in(streams_of[6], 1), 0, 1),
        "down_mask": place_ends((jax.random.randint(streams_of[7], (HID // BLK, D // BLK), 0, 2) < 1).astype(jnp.int32), jax.random.fold_in(streams_of[7], 1), 0, 1),
    }


def masked(weight, block_mask):
    block_rows, block_cols = block_mask.shape
    total_rows, total_cols = weight.shape
    shaped = weight.reshape(block_rows, total_rows // block_rows, block_cols, total_cols // block_cols)
    return (shaped * block_mask.astype(weight.dtype)[:, None, :, None]).reshape(total_rows, total_cols)


def reference(tokens, cotangent, gate_weight, up_weight, down_weight, gate_mask, up_mask, down_mask):
    gate_eff = masked(gate_weight, gate_mask)
    up_eff = masked(up_weight, up_mask)
    down_eff = masked(down_weight, down_mask)
    gate = jnp.dot(tokens, gate_eff, preferred_element_type=jnp.float32)
    up = jnp.dot(tokens, up_eff, preferred_element_type=jnp.float32)
    sigmoid_gate = jax.nn.sigmoid(gate)
    activated = gate * sigmoid_gate
    hidden = (activated * up).astype(jnp.bfloat16)
    output = jnp.dot(hidden, down_eff, preferred_element_type=jnp.float32).astype(jnp.bfloat16)
    d_hidden = jnp.dot(cotangent, down_eff.T, preferred_element_type=jnp.float32)
    d_gate = (d_hidden * up * sigmoid_gate * (1.0 + gate * (1.0 - sigmoid_gate))).astype(jnp.bfloat16)
    d_up = (d_hidden * activated).astype(jnp.bfloat16)
    grad_down = masked(jnp.dot(hidden.T, cotangent, preferred_element_type=jnp.float32), down_mask).astype(jnp.bfloat16)
    grad_gate = masked(jnp.dot(tokens.T, d_gate, preferred_element_type=jnp.float32), gate_mask).astype(jnp.bfloat16)
    grad_up = masked(jnp.dot(tokens.T, d_up, preferred_element_type=jnp.float32), up_mask).astype(jnp.bfloat16)
    d_total = jnp.dot(d_gate, gate_eff.T, preferred_element_type=jnp.float32) + jnp.dot(d_up, up_eff.T, preferred_element_type=jnp.float32)
    d_tokens = d_total.astype(jnp.bfloat16)
    return (output, d_tokens, grad_gate, grad_up, grad_down)
```

```python
import functools

import jax
import jax.numpy as jnp
from jax import lax
from jax.experimental import pallas as pl
from jax.experimental.pallas import tpu as pltpu
from jax.sharding import PartitionSpec as P

BLK = 128
F32 = jnp.float32
BF16 = jnp.bfloat16
LIMIT = 48 * 1024 * 1024


def tile_of(width):
    for tile in (512, 256, 128):
        if width % tile == 0:
            return tile
    return width


def params():
    return pltpu.CompilerParams(
        vmem_limit_bytes=LIMIT
    )


def cost(*arrays, flops):
    moved = sum(a.size * jnp.dtype(a.dtype).itemsize for a in arrays)
    return pl.CostEstimate(flops=flops, bytes_accessed=moved, transcendentals=0)


def keep_blocks(value, mask_ref, row0, col0):
    rows, cols = value.shape
    strips = []
    for i in range(rows // BLK):
        pieces = []
        for j in range(cols // BLK):
            keep = mask_ref[row0 + i, col0 + j].astype(F32)
            piece = value[i * BLK : (i + 1) * BLK, j * BLK : (j + 1) * BLK]
            pieces.append(piece * jnp.full((BLK, BLK), keep, F32).astype(value.dtype))
        strips.append(jnp.concatenate(pieces, axis=1))
    return jnp.concatenate(strips, axis=0)


def dot(a, b, dims):
    return lax.dot_general(a, b, (dims, ((), ())), preferred_element_type=F32)


NN = ((1,), (0,))
NT = ((1,), (1,))
TN = ((0,), (0,))

SMEM = functools.partial(pl.BlockSpec, memory_space=pltpu.SMEM)


def gate_up_kernel(first, wide, gm_ref, um_ref, x_ref, g_ref, u_ref, keep_ref, send_ref):
    half = x_ref.shape[0] // 2
    col0 = (first + pl.program_id(0)) * wide
    for slot, (m_ref, w_ref) in enumerate(((gm_ref, g_ref), (um_ref, u_ref))):
        part = dot(x_ref[...], keep_blocks(w_ref[...], m_ref, 0, col0), NN)
        keep_ref[slot] = part[:half]
        send_ref[slot] = part[half:]


def gate_up(x, gate, up, gm, um, start, width):
    tokens, depth = x.shape
    tile = tile_of(width)
    first = start // tile
    weight = pl.BlockSpec((depth, tile), lambda i: (0, first + i))
    out = jax.ShapeDtypeStruct((2, tokens // 2, width), F32)
    return pl.pallas_call(
        functools.partial(gate_up_kernel, first, tile // BLK),
        grid=(width // tile,),
        in_specs=[SMEM(), SMEM(), pl.BlockSpec((tokens, depth), lambda i: (0, 0)), weight, weight],
        out_specs=[pl.BlockSpec((2, tokens // 2, tile), lambda i: (0, 0, i))] * 2,
        out_shape=[out, out],
        compiler_params=params(),
        cost_estimate=cost(x, out, out, out, flops=4 * tokens * depth * width),
        name="gate_up",
    )(gm, um, x, gate, up)


def d_hidden_kernel(first, tall, m_ref, x_ref, w_ref, keep_ref, send_ref):
    half = x_ref.shape[0] // 2
    row0 = (first + pl.program_id(0)) * tall
    part = dot(x_ref[...], keep_blocks(w_ref[...], m_ref, row0, 0), NT)
    keep_ref[0] = part[:half]
    send_ref[0] = part[half:]


def d_hidden(x, down, dm, start, width):
    tokens, depth = x.shape
    tile = tile_of(width)
    first = start // tile
    out = jax.ShapeDtypeStruct((1, tokens // 2, width), F32)
    return pl.pallas_call(
        functools.partial(d_hidden_kernel, first, tile // BLK),
        grid=(width // tile,),
        in_specs=[
            SMEM(),
            pl.BlockSpec((tokens, depth), lambda i: (0, 0)),
            pl.BlockSpec((tile, depth), lambda i: (first + i, 0)),
        ],
        out_specs=[pl.BlockSpec((1, tokens // 2, tile), lambda i: (0, 0, i))] * 2,
        out_shape=[out, out],
        compiler_params=params(),
        cost_estimate=cost(x, out, out, flops=2 * tokens * depth * width),
        name="d_hidden",
    )(dm, x, down)


def halves_specs(groups, half, tile, steps):
    low = pl.BlockSpec((groups, half, tile), lambda i: (0, 0, jnp.minimum(i, steps - 1)))
    high = pl.BlockSpec((groups, half, tile), lambda i: (0, 0, jnp.maximum(i - steps, 0)))
    return [low, low, high, high]


def pick(steps, refs, slot, low):
    a, b = (refs[0], refs[1]) if low else (refs[2], refs[3])
    return jnp.concatenate([a[slot], b[slot]], axis=0)


def both(steps, body):
    i = pl.program_id(0)

    @pl.when(i < steps)
    def _():
        body(True)

    @pl.when(i >= steps)
    def _():
        body(False)


def down_kernel(steps, tall, m_ref, c_ref, w_ref, *rest):
    refs, (out_ref, grad_ref) = rest[:4], rest[4:]
    i = pl.program_id(0)

    @pl.when(i == 0)
    def _():
        out_ref[...] = jnp.zeros_like(out_ref)

    def body(low):
        hid = pick(steps, refs, 0, low)
        out_ref[...] += dot(hid, keep_blocks(w_ref[...], m_ref, i * tall, 0), NN)
        grad = dot(hid, c_ref[...], TN)
        grad_ref[...] = keep_blocks(grad, m_ref, i * tall, 0).astype(BF16)

    both(steps, body)


def down_side(cot, down, dm, pieces):
    tokens, depth = cot.shape
    hid = down.shape[0]
    width = hid // 2
    tile = tile_of(width)
    steps = width // tile
    rows = pl.BlockSpec((tile, depth), lambda i: (i, 0))
    return pl.pallas_call(
        functools.partial(down_kernel, steps, tile // BLK),
        grid=(2 * steps,),
        in_specs=[SMEM(), pl.BlockSpec((tokens, depth), lambda i: (0, 0)), rows]
        + halves_specs(1, tokens // 2, tile, steps),
        out_specs=[pl.BlockSpec((tokens, depth), lambda i: (0, 0)), rows],
        out_shape=[
            jax.ShapeDtypeStruct((tokens, depth), F32),
            jax.ShapeDtypeStruct((hid, depth), BF16),
        ],
        compiler_params=params(),
        cost_estimate=cost(cot, down, down, *pieces, flops=4 * tokens * depth * hid),
        name="down_side",
    )(dm, cot, down, *pieces)


def d_tokens_kernel(steps, wide, gm_ref, um_ref, g_ref, u_ref, *rest):
    refs, out_ref = rest[:4], rest[4]
    i = pl.program_id(0)

    @pl.when(i == 0)
    def _():
        out_ref[...] = jnp.zeros_like(out_ref)

    def body(low):
        out_ref[...] += dot(
            pick(steps, refs, 0, low), keep_blocks(g_ref[...], gm_ref, 0, i * wide), NT
        ) + dot(pick(steps, refs, 1, low), keep_blocks(u_ref[...], um_ref, 0, i * wide), NT)

    both(steps, body)


def d_tokens_part(gate, up, gm, um, pieces):
    depth, hid = gate.shape
    tokens = 2 * pieces[0].shape[1]
    width = hid // 2
    tile = tile_of(width)
    steps = width // tile
    weight = pl.BlockSpec((depth, tile), lambda i: (0, i))
    return pl.pallas_call(
        functools.partial(d_tokens_kernel, steps, tile // BLK),
        grid=(2 * steps,),
        in_specs=[SMEM(), SMEM(), weight, weight] + halves_specs(2, tokens // 2, tile, steps),
        out_specs=pl.BlockSpec((tokens, depth), lambda i: (0, 0)),
        out_shape=jax.ShapeDtypeStruct((tokens, depth), F32),
        compiler_params=params(),
        cost_estimate=cost(gate, up, *pieces, flops=4 * tokens * depth * hid),
        name="d_tokens",
    )(gm, um, gate, up, *pieces)


def grads_kernel(steps, wide, gm_ref, um_ref, xt_ref, *rest):
    refs, outs = rest[:4], rest[4:]
    i = pl.program_id(0)

    def body(low):
        for slot, (m_ref, out_ref) in enumerate(zip((gm_ref, um_ref), outs)):
            grad = dot(xt_ref[...], pick(steps, refs, slot, low), NN)
            out_ref[...] = keep_blocks(grad, m_ref, 0, i * wide).astype(BF16)

    both(steps, body)


def weight_grads(xt, gm, um, pieces):
    depth, tokens = xt.shape
    width = pieces[0].shape[2]
    tile = tile_of(width)
    steps = width // tile
    out = jax.ShapeDtypeStruct((depth, 2 * width), BF16)
    return pl.pallas_call(
        functools.partial(grads_kernel, steps, tile // BLK),
        grid=(2 * steps,),
        in_specs=[SMEM(), SMEM(), pl.BlockSpec((depth, tokens), lambda i: (0, 0))]
        + halves_specs(2, tokens // 2, tile, steps),
        out_specs=[pl.BlockSpec((depth, tile), lambda i: (0, i))] * 2,
        out_shape=[out, out],
        compiler_params=params(),
        cost_estimate=cost(out, out, *pieces, flops=8 * tokens * depth * width),
        name="weight_grads",
    )(gm, um, xt, *pieces)


def move_kernel(index_ref, from_ref, to_ref):
    to_ref[...] = from_ref[...]


def ordered(value, index):
    count, width = index.shape[0], value.shape[1]
    block = value.shape[0] // count
    return pl.pallas_call(
        move_kernel,
        grid_spec=pltpu.PrefetchScalarGridSpec(
            num_scalar_prefetch=1,
            grid=(count,),
            in_specs=[pl.BlockSpec((block, width), lambda i, index: (index[i], 0))],
            out_specs=pl.BlockSpec((block, width), lambda i, index: (i, 0)),
        ),
        out_shape=jax.ShapeDtypeStruct(value.shape, value.dtype),
        compiler_params=params(),
        cost_estimate=cost(value, value, flops=0),
        name="ordered",
    )(index, value)


def swap(value, bit, rows):
    return lax.ppermute(value, "row", [(i, i ^ bit) for i in range(rows)])


def reduce_rows(keep, send, order, rows):
    groups, half, width = keep.shape
    total = keep + swap(send, 1, rows)
    left = sorted(order, reverse=True)
    total = total.reshape((groups,) + (2,) * len(left) + (half * 2 // rows, width))
    for bit in order:
        axis = 1 + left.index(bit)
        away = lax.index_in_dim(total, 1, axis, keepdims=False).astype(BF16)
        stay = lax.index_in_dim(total, 0, axis, keepdims=False)
        total = stay + swap(away, bit, rows).astype(F32)
        left.remove(bit)
    return total


def gather_rows(share, order, rows):
    groups, block, width = share.shape
    have = []
    value = share
    for bit in reversed(order):
        have = sorted(have + [bit], reverse=True)
        value = jnp.stack([value, swap(value, bit, rows)], axis=1 + have.index(bit))
    value = value.reshape(groups, block * rows // 2, width)
    return value, swap(value, 1, rows)


def per_device(
    tokens, cotangent, gate_weight, up_weight, down_weight, gate_mask, up_mask, down_mask
):
    rows = lax.axis_size("row")
    me = lax.axis_index("row")
    hid = down_weight.shape[0]
    width = hid // 2
    bits = [1 << b for b in range(1, rows.bit_length() - 1)]
    orders = (bits, bits[::-1])

    place = jnp.arange(rows)
    half_rows = rows // 2
    relative = ((place % half_rows) * 2 + place // half_rows) ^ me
    other = place ^ me
    back = (other % 2) * half_rows + other // 2

    cot = ordered(lax.all_gather(cotangent, "col", axis=0, tiled=True), relative)
    x = ordered(lax.all_gather(tokens, "col", axis=0, tiled=True), relative)
    xt = x.T

    d_hid = []
    for k, order in enumerate(orders):
        keep, send = d_hidden(cot, down_weight, down_mask, k * width, width)
        d_hid.append(reduce_rows(keep, send, order, rows)[0])
    hidden_pieces, grad_pieces = [], []
    shares = []
    for k, order in enumerate(orders):
        keep, send = gate_up(
            x, gate_weight, up_weight, gate_mask, up_mask, k * width, width
        )
        shares.append(reduce_rows(keep, send, order, rows))
    for k, order in enumerate(orders):
        gate, up = shares[k][0], shares[k][1]
        hidden = (gate * jax.nn.sigmoid(gate) * up).astype(BF16)
        hidden_pieces += gather_rows(hidden[None], order, rows)
    for k, order in enumerate(orders):
        gate, up, dh = shares[k][0], shares[k][1], d_hid[k]
        s = jax.nn.sigmoid(gate)
        d_gate = (dh * up * s * (1.0 + gate * (1.0 - s))).astype(BF16)
        d_up = (dh * (gate * s)).astype(BF16)
        grad_pieces += gather_rows(jnp.stack([d_gate, d_up]), order, rows)

    def spread(part):
        return lax.psum_scatter(
            ordered(part, back), "col", scatter_dimension=0, tiled=True
        ).astype(BF16)

    part, grad_down = down_side(cot, down_weight, down_mask, hidden_pieces)
    output = spread(part)
    d_tokens = spread(d_tokens_part(gate_weight, up_weight, gate_mask, up_mask, grad_pieces))
    grad_gate, grad_up = weight_grads(xt, gate_mask, up_mask, grad_pieces)
    return (output, d_tokens, grad_gate, grad_up, grad_down)


def solution(mesh):
    model, weight, down = P("col", "row"), P("row", "col"), P("col", "row")
    return jax.shard_map(
        per_device,
        mesh=mesh,
        in_specs=(model, model, weight, weight, down, weight, weight, down),
        out_specs=(model, model, weight, weight, down),
        check_vma=False,
    )
```

```python
import functools

import jax
import jax.numpy as jnp
from jax import lax
from jax.experimental import pallas as pl
from jax.experimental.pallas import tpu as pltpu
from jax.sharding import PartitionSpec as P

BLK = 128
F32 = jnp.float32
BF16 = jnp.bfloat16
LIMIT = 48 * 1024 * 1024


def tile_of(width):
    for tile in (512, 256, 128):
        if width % tile == 0:
            return tile
    return width


def params():
    return pltpu.CompilerParams(
        vmem_limit_bytes=LIMIT
    )


def cost(*arrays, flops):
    moved = sum(a.size * jnp.dtype(a.dtype).itemsize for a in arrays)
    return pl.CostEstimate(flops=flops, bytes_accessed=moved, transcendentals=0)


def keep_blocks(value, mask_ref, row0, col0):
    rows, cols = value.shape
    strips = []
    for i in range(rows // BLK):
        pieces = []
        for j in range(cols // BLK):
            keep = mask_ref[row0 + i, col0 + j].astype(F32)
            piece = value[i * BLK : (i + 1) * BLK, j * BLK : (j + 1) * BLK]
            pieces.append(piece * jnp.full((BLK, BLK), keep, F32).astype(value.dtype))
        strips.append(jnp.concatenate(pieces, axis=1))
    return jnp.concatenate(strips, axis=0)


def dot(a, b, dims):
    return lax.dot_general(a, b, (dims, ((), ())), preferred_element_type=F32)


NN = ((1,), (0,))
NT = ((1,), (1,))
TN = ((0,), (0,))

SMEM = functools.partial(pl.BlockSpec, memory_space=pltpu.SMEM)


def gate_up_kernel(first, wide, gm_ref, um_ref, x_ref, g_ref, u_ref, keep_ref, send_ref):
    half = x_ref.shape[0] // 2
    col0 = (first + pl.program_id(0)) * wide
    for slot, (m_ref, w_ref) in enumerate(((gm_ref, g_ref), (um_ref, u_ref))):
        part = dot(x_ref[...], keep_blocks(w_ref[...], m_ref, 0, col0), NN)
        keep_ref[slot] = part[:half]
        send_ref[slot] = part[half:]


def gate_up(x, gate, up, gm, um, start, width):
    tokens, depth = x.shape
    tile = tile_of(width)
    first = start // tile
    weight = pl.BlockSpec((depth, tile), lambda i: (0, first + i))
    out = jax.ShapeDtypeStruct((2, tokens // 2, width), F32)
    return pl.pallas_call(
        functools.partial(gate_up_kernel, first, tile // BLK),
        grid=(width // tile,),
        in_specs=[SMEM(), SMEM(), pl.BlockSpec((tokens, depth), lambda i: (0, 0)), weight, weight],
        out_specs=[pl.BlockSpec((2, tokens // 2, tile), lambda i: (0, 0, i))] * 2,
        out_shape=[out, out],
        compiler_params=params(),
        cost_estimate=cost(x, out, out, out, flops=4 * tokens * depth * width),
        name="gate_up",
    )(gm, um, x, gate, up)


def d_hidden_kernel(first, tall, m_ref, x_ref, w_ref, keep_ref, send_ref):
    half = x_ref.shape[0] // 2
    row0 = (first + pl.program_id(0)) * tall
    part = dot(x_ref[...], keep_blocks(w_ref[...], m_ref, row0, 0), NT)
    keep_ref[0] = part[:half]
    send_ref[0] = part[half:]


def d_hidden(x, down, dm, start, width):
    tokens, depth = x.shape
    tile = tile_of(width)
    first = start // tile
    out = jax.ShapeDtypeStruct((1, tokens // 2, width), F32)
    return pl.pallas_call(
        functools.partial(d_hidden_kernel, first, tile // BLK),
        grid=(width // tile,),
        in_specs=[
            SMEM(),
            pl.BlockSpec((tokens, depth), lambda i: (0, 0)),
            pl.BlockSpec((tile, depth), lambda i: (first + i, 0)),
        ],
        out_specs=[pl.BlockSpec((1, tokens // 2, tile), lambda i: (0, 0, i))] * 2,
        out_shape=[out, out],
        compiler_params=params(),
        cost_estimate=cost(x, out, out, flops=2 * tokens * depth * width),
        name="d_hidden",
    )(dm, x, down)


def halves_specs(groups, half, tile, steps):
    low = pl.BlockSpec((groups, half, tile), lambda i: (0, 0, jnp.minimum(i, steps - 1)))
    high = pl.BlockSpec((groups, half, tile), lambda i: (0, 0, jnp.maximum(i - steps, 0)))
    return [low, low, high, high]


def pick(steps, refs, slot, low):
    a, b = (refs[0], refs[1]) if low else (refs[2], refs[3])
    return jnp.concatenate([a[slot], b[slot]], axis=0)


def both(steps, body):
    i = pl.program_id(0)

    @pl.when(i < steps)
    def _():
        body(True)

    @pl.when(i >= steps)
    def _():
        body(False)


def down_kernel(steps, tall, m_ref, c_ref, w_ref, *rest):
    refs, (out_ref, grad_ref) = rest[:4], rest[4:]
    i = pl.program_id(0)

    @pl.when(i == 0)
    def _():
        out_ref[...] = jnp.zeros_like(out_ref)

    def body(low):
        hid = pick(steps, refs, 0, low)
        out_ref[...] += dot(hid, keep_blocks(w_ref[...], m_ref, i * tall, 0), NN)
        grad = dot(hid, c_ref[...], TN)
        grad_ref[...] = keep_blocks(grad, m_ref, i * tall, 0).astype(BF16)

    both(steps, body)


def down_side(cot, down, dm, pieces):
    tokens, depth = cot.shape
    hid = down.shape[0]
    width = hid // 2
    tile = tile_of(width)
    steps = width // tile
    rows = pl.BlockSpec((tile, depth), lambda i: (i, 0))
    return pl.pallas_call(
        functools.partial(down_kernel, steps, tile // BLK),
        grid=(2 * steps,),
        in_specs=[SMEM(), pl.BlockSpec((tokens, depth), lambda i: (0, 0)), rows]
        + halves_specs(1, tokens // 2, tile, steps),
        out_specs=[pl.BlockSpec((tokens, depth), lambda i: (0, 0)), rows],
        out_shape=[
            jax.ShapeDtypeStruct((tokens, depth), F32),
            jax.ShapeDtypeStruct((hid, depth), BF16),
        ],
        compiler_params=params(),
        cost_estimate=cost(cot, down, down, *pieces, flops=4 * tokens * depth * hid),
        name="down_side",
    )(dm, cot, down, *pieces)


def d_tokens_kernel(steps, wide, gm_ref, um_ref, g_ref, u_ref, *rest):
    refs, out_ref = rest[:4], rest[4]
    i = pl.program_id(0)

    @pl.when(i == 0)
    def _():
        out_ref[...] = jnp.zeros_like(out_ref)

    def body(low):
        out_ref[...] += dot(
            pick(steps, refs, 0, low), keep_blocks(g_ref[...], gm_ref, 0, i * wide), NT
        ) + dot(pick(steps, refs, 1, low), keep_blocks(u_ref[...], um_ref, 0, i * wide), NT)

    both(steps, body)


def d_tokens_part(gate, up, gm, um, pieces):
    depth, hid = gate.shape
    tokens = 2 * pieces[0].shape[1]
    width = hid // 2
    tile = tile_of(width)
    steps = width // tile
    weight = pl.BlockSpec((depth, tile), lambda i: (0, i))
    return pl.pallas_call(
        functools.partial(d_tokens_kernel, steps, tile // BLK),
        grid=(2 * steps,),
        in_specs=[SMEM(), SMEM(), weight, weight] + halves_specs(2, tokens // 2, tile, steps),
        out_specs=pl.BlockSpec((tokens, depth), lambda i: (0, 0)),
        out_shape=jax.ShapeDtypeStruct((tokens, depth), F32),
        compiler_params=params(),
        cost_estimate=cost(gate, up, *pieces, flops=4 * tokens * depth * hid),
        name="d_tokens",
    )(gm, um, gate, up, *pieces)


def grads_kernel(steps, wide, gm_ref, um_ref, xt_ref, *rest):
    refs, outs = rest[:4], rest[4:]
    i = pl.program_id(0)

    def body(low):
        for slot, (m_ref, out_ref) in enumerate(zip((gm_ref, um_ref), outs)):
            grad = dot(xt_ref[...], pick(steps, refs, slot, low), NN)
            out_ref[...] = keep_blocks(grad, m_ref, 0, i * wide).astype(BF16)

    both(steps, body)


def weight_grads(xt, gm, um, pieces):
    depth, tokens = xt.shape
    width = pieces[0].shape[2]
    tile = tile_of(width)
    steps = width // tile
    out = jax.ShapeDtypeStruct((depth, 2 * width), BF16)
    return pl.pallas_call(
        functools.partial(grads_kernel, steps, tile // BLK),
        grid=(2 * steps,),
        in_specs=[SMEM(), SMEM(), pl.BlockSpec((depth, tokens), lambda i: (0, 0))]
        + halves_specs(2, tokens // 2, tile, steps),
        out_specs=[pl.BlockSpec((depth, tile), lambda i: (0, i))] * 2,
        out_shape=[out, out],
        compiler_params=params(),
        cost_estimate=cost(out, out, *pieces, flops=8 * tokens * depth * width),
        name="weight_grads",
    )(gm, um, xt, *pieces)


def move_kernel(index_ref, from_ref, to_ref):
    to_ref[...] = from_ref[...]


def ordered(value, index):
    count, width = index.shape[0], value.shape[1]
    block = value.shape[0] // count
    return pl.pallas_call(
        move_kernel,
        grid_spec=pltpu.PrefetchScalarGridSpec(
            num_scalar_prefetch=1,
            grid=(count,),
            in_specs=[pl.BlockSpec((block, width), lambda i, index: (index[i], 0))],
            out_specs=pl.BlockSpec((block, width), lambda i, index: (i, 0)),
        ),
        out_shape=jax.ShapeDtypeStruct(value.shape, value.dtype),
        compiler_params=params(),
        cost_estimate=cost(value, value, flops=0),
        name="ordered",
    )(index, value)


def swap(value, bit, rows):
    return lax.ppermute(value, "row", [(i, i ^ bit) for i in range(rows)])


def split(total, bits, bit):
    axis = 1 + bits.index(bit)
    away = lax.index_in_dim(total, 1, axis, keepdims=False).astype(BF16)
    return lax.index_in_dim(total, 0, axis, keepdims=False), away


def pair_rows(keep, send, order, rows):
    groups, half, width = keep.shape
    total = keep + swap(send, 1, rows)
    bits = sorted(order, reverse=True)
    total = total.reshape((groups,) + (2,) * len(bits) + (half * 2 // rows, width))
    return split(total, bits, order[0])


def reduce_rows(stay, away, order, rows):
    for k, bit in enumerate(order):
        total = stay + swap(away, bit, rows).astype(F32)
        if k + 1 < len(order):
            stay, away = split(total, sorted(order[k + 1 :], reverse=True), order[k + 1])
    return total


def gather_rows(share, order, rows, tie=None):
    groups, block, width = share.shape
    have = []
    value = share
    for bit in reversed(order):
        have = sorted(have + [bit], reverse=True)
        other = swap(value, bit, rows)
        if tie is not None and bit == order[0]:
            other, tie = lax.optimization_barrier((other, tie))
        value = jnp.stack([value, other], axis=1 + have.index(bit))
    value = value.reshape(groups, block * rows // 2, width)
    return (value, swap(value, 1, rows)), tie


def per_device(
    tokens, cotangent, gate_weight, up_weight, down_weight, gate_mask, up_mask, down_mask
):
    rows = lax.axis_size("row")
    me = lax.axis_index("row")
    hid = down_weight.shape[0]
    width = hid // 2
    bits = [1 << b for b in range(1, rows.bit_length() - 1)]
    orders = (bits, bits[::-1])

    place = jnp.arange(rows)
    half_rows = rows // 2
    relative = ((place % half_rows) * 2 + place // half_rows) ^ me
    other = place ^ me
    back = (other % 2) * half_rows + other // 2

    cot = ordered(lax.all_gather(cotangent, "col", axis=0, tiled=True), relative)
    x = ordered(lax.all_gather(tokens, "col", axis=0, tiled=True), relative)
    xt = x.T

    stays, aways = [], []
    for k, order in enumerate(orders):
        keep, send = d_hidden(cot, down_weight, down_mask, k * width, width)
        stay, away = pair_rows(keep, send, order, rows)
        stays.append(stay)
        aways.append(away)
    x, aways = lax.optimization_barrier((x, aways))
    d_hid = [
        reduce_rows(stay, away, order, rows)[0]
        for stay, away, order in zip(stays, aways, orders)
    ]
    hidden_pieces, grad_pieces = [], []
    shares = []
    for k, order in enumerate(orders):
        keep, send = gate_up(
            x, gate_weight, up_weight, gate_mask, up_mask, k * width, width
        )
        shares.append(reduce_rows(*pair_rows(keep, send, order, rows), order, rows))
    for k, order in enumerate(orders):
        gate, up = shares[k][0], shares[k][1]
        hidden = (gate * jax.nn.sigmoid(gate) * up).astype(BF16)
        hidden_pieces += gather_rows(hidden[None], order, rows)[0]
    part, grad_down = down_side(cot, down_weight, down_mask, hidden_pieces)
    for k, order in enumerate(orders):
        gate, up, dh = shares[k][0], shares[k][1], d_hid[k]
        s = jax.nn.sigmoid(gate)
        d_gate = (dh * up * s * (1.0 + gate * (1.0 - s))).astype(BF16)
        d_up = (dh * (gate * s)).astype(BF16)
        pieces, part = gather_rows(jnp.stack([d_gate, d_up]), order, rows, part)
        grad_pieces += pieces

    def spread(part):
        return lax.psum_scatter(
            ordered(part, back), "col", scatter_dimension=0, tiled=True
        ).astype(BF16)

    output = spread(part)
    d_tokens = spread(d_tokens_part(gate_weight, up_weight, gate_mask, up_mask, grad_pieces))
    grad_gate, grad_up = weight_grads(xt, gate_mask, up_mask, grad_pieces)
    return (output, d_tokens, grad_gate, grad_up, grad_down)


def solution(mesh):
    model, weight, down = P("col", "row"), P("row", "col"), P("col", "row")
    return jax.shard_map(
        per_device,
        mesh=mesh,
        in_specs=(model, model, weight, weight, down, weight, weight, down),
        out_specs=(model, model, weight, weight, down),
        check_vma=False,
    )
```
